32 devices in a mesh: ka: 8 (over z, x), ba: 4 (over y, core).
Axes of the slice: x: 2, y: 2, z: 4, core: 2. Of those that a mesh axis runs over, the one named last changes fastest.
Arguments:
- density: float32 [2, 2048, 4096], P(None, 'ka', 'ba'), may hold values from -6 to 6
- h_bands: float32 [2, 2048, 4096], P(None, ('ka', 'ba')), may hold values from -0.75 to 0.75
- coupling: bfloat16 [16, 4, 128, 128], P('ka'), may hold values from -0.03125 to 0.03125
- donors: int32 [16, 4], P('ka'), may hold values from 0 to 15, as said below
- counts: int32 [16], P('ka'), may hold values from 2 to 4, as said below
Outputs:
- evolved: float32 [2, 2048, 4096], P(None, 'ka', 'ba')
The draws below stay inside these ranges and needn't reach their ends.
Inputs may be any that keep to these rules, and one draw needn't show every extreme that they name: donors[t] holds 4 different tiles, each within 2 tiles of t in the cyclic order of the 16 tiles; donors[t, 0] = t. `counts`: some tile uses all 4 slots.
All inputs are finite; a program needn't handle non-finite values.
Results may differ from the reference program's by a relative error of at most 0.0013.
Values may be sent and summed in bfloat16 or wider, within the bound.
No kernel may reach another device: no remote copies, remote signals or barrier semaphores. Data moves between devices by JAX's collectives and lax.ppermute only.
A program may use at most 64 MiB of HBM per device.

```python
import jax
import jax.numpy as jnp
from jax import lax

NB = 64
TILE = 128
ND = 4
REACH = 2
PAIRS = 4096
TILES = 16
MOM = 2048


def draw_donors(key, part):
    subkeys = jax.random.split(key, TILES)
    others = 2 * REACH

    def single_row(subkey):
        shuffled = jax.random.permutation(subkey, others).astype(jnp.int32)
        nearby = jnp.where(shuffled < REACH, shuffled - REACH, shuffled - REACH + 1)
        return jnp.concatenate([jnp.zeros((1,), jnp.int32), nearby[:ND - 1]])
    offsets = jax.vmap(single_row)(subkeys)
    return ((jnp.arange(TILES, dtype=jnp.int32)[:, None] + offsets) % TILES).astype(jnp.int32)


def draw_counts(key, part):
    key_values = jax.random.fold_in(key, 11)
    key_place = jax.random.fold_in(key, 23)
    values = jax.random.randint(key_values, (TILES,), 2, ND + 1).astype(jnp.int32)
    where_full = jax.random.randint(key_place, (), 0, TILES)
    return values.at[where_full].set(ND).astype(jnp.int32)


def steps_of(own_key, extent, cuts, low, top_value):
    gain, own = 1.0, jax.random.fold_in(own_key, 6)
    for dim, shards_of in cuts:
        draws = jnp.exp(jax.random.uniform(jax.random.fold_in(own, dim), (shards_of,), jnp.float32, low / len(cuts), top_value / len(cuts)))
        gain = gain * jnp.repeat(draws, extent[dim] // shards_of).reshape([-1 if axis == dim else 1 for axis in range(len(extent))])
    return gain


def centred(stream_key, extent, scale, most, shards=(), kind=jnp.bfloat16):
    entries = jax.random.normal(stream_key, extent, jnp.float32) * scale
    if len(shards) > 0:
        entries = steps_of(stream_key, extent, shards, -0.22, 0.18) * entries
    return jnp.clip(entries, min=-most, max=most).astype(kind)


def setup_inputs(seed: int = 0) -> dict:
    keys = jax.random.split(jax.random.key(seed), 6)
    return {
        "density": centred(keys[0], (2, MOM, PAIRS), 1.0, 6.0, ((1, 8), (2, 4)), jnp.float32),
        "h_bands": centred(keys[1], (2, MOM, PAIRS), 0.125, 0.75, ((1, 32),), jnp.float32),
        "coupling": centred(keys[2], (TILES, ND, TILE, TILE), (ND * TILE * NB) ** -0.5, 0.03125, ((0, 8),)),
        "donors": draw_donors(jax.random.fold_in(keys[5], 71), 0),
        "counts": draw_counts(jax.random.fold_in(keys[5], 71), 0),
    }


step_size = 0.25


def commute(hamilton, state):
    count = state.shape[1]
    h_real = hamilton[0].reshape(count, NB, NB)
    h_imag = hamilton[1].reshape(count, NB, NB)
    s_real = state[0].reshape(count, NB, NB)
    s_imag = state[1].reshape(count, NB, NB)

    def product(left, right):
        return jnp.einsum("mab,mbc->mac", left, right, precision=lax.Precision.HIGHEST)

    c_real = product(h_real, s_real) - product(h_imag, s_imag) - product(s_real, h_real) + product(s_imag, h_imag)
    c_imag = product(h_real, s_imag) + product(h_imag, s_real) - product(s_real, h_imag) - product(s_imag, h_real)
    return jnp.stack([c_imag, -c_real]).reshape(2, count, NB * NB)


def reference(density, h_bands, coupling, donors, counts):
    active = (jnp.arange(ND, dtype=jnp.int32)[None, :] < counts[:, None]).astype(jnp.bfloat16)
    masked = coupling * active[:, :, None, None]

    def self_energy(state):
        rounded = state.astype(jnp.bfloat16).reshape(2, TILES, TILE, PAIRS)

        def single(pair):
            weights, indices = pair
            picked = rounded[:, indices].astype(jnp.float32)
            return jnp.einsum("skq,csqp->ckp", weights.astype(jnp.float32), picked, precision=lax.Precision.HIGHEST)

        result = lax.map(single, (masked, donors))
        return -jnp.transpose(result, (1, 0, 2, 3)).reshape(2, MOM, PAIRS)

    def tendency(state):
        return commute(h_bands + self_energy(state), state)

    rate_one = tendency(density)
    middle = density + 0.5 * step_size * rate_one
    rate_two = tendency(middle)
    return density + step_size * rate_two
```

```python
import functools

import jax
import jax.numpy as jnp
from jax import lax
from jax.experimental import pallas as pl
from jax.experimental.pallas import tpu as pltpu
from jax.sharding import PartitionSpec as P

NB = 64
TILE = 128
ND = 4
REACH = 2
LANE = 2 * NB
SPAN = (2 * REACH + 1) * TILE

step_size = 0.25
f32, bf16, i16, i32 = jnp.float32, jnp.bfloat16, jnp.int16, jnp.int32
SMEM = pl.BlockSpec(memory_space=pltpu.SMEM)
VMEM = pl.BlockSpec(memory_space=pltpu.VMEM)


def call(kernel, out, scratch=(), specs=None, n_in=0, flops=0, moved=0):
    return pl.pallas_call(
        kernel,
        out_shape=out,
        in_specs=specs if specs is not None else [SMEM] + [VMEM] * n_in,
        scratch_shapes=scratch,
        compiler_params=pltpu.CompilerParams(vmem_limit_bytes=48 * 2**20),
        cost_estimate=pl.CostEstimate(flops=flops, bytes_accessed=moved, transcendentals=0),
    )


def half_lanes(shape):
    return lax.broadcasted_iota(i32, shape, 1) < NB


def rows_of(real, imag):
    low = half_lanes(real.shape)
    even = jnp.where(low, real, pltpu.roll(imag, NB, 1))
    odd = jnp.where(low, pltpu.roll(real, NB, 1), imag)
    return even, odd


def parts_of(even, odd):
    low = half_lanes(even.shape)
    real = jnp.where(low, even, pltpu.roll(odd, NB, 1))
    imag = jnp.where(low, pltpu.roll(even, NB, 1), odd)
    return real, imag


def encode(values, peak):
    power = jnp.ceil(jnp.log2(jnp.maximum(peak, 1e-30)))
    scale = jnp.exp2(15.0 - power)
    codes = [jnp.clip(jnp.round(v * scale), -32767.0, 32767.0).astype(i32).astype(i16) for v in values]
    return codes, power


def decode_scale(power):
    return jnp.exp2(power.astype(i32).astype(f32) - 15.0)


def round_kernel(place, density, mine, other):
    x = place[0]
    width = density.shape[2] // 2
    for out, half in ((mine, x), (other, 1 - x)):
        for t in range(width // LANE):
            cols = pl.ds(pl.multiple_of(half * width + t * LANE, LANE), LANE)
            even, odd = rows_of(density[0, :, cols], density[1, :, cols])
            out[:, 2 * t * LANE : (2 * t + 1) * LANE] = even.astype(bf16)
            out[:, (2 * t + 1) * LANE : (2 * t + 2) * LANE] = odd.astype(bf16)


def split_kernel(place, density, *outs):
    j = place[1]
    rows = outs[0].shape[0]
    for k, out in enumerate(outs):
        at = pl.ds(pl.multiple_of((j ^ k) * rows, rows), rows)
        for t in range(density.shape[2] // LANE):
            cols = slice(t * LANE, (t + 1) * LANE)
            even, odd = rows_of(density[0, at, cols], density[1, at, cols])
            out[:, 2 * t * LANE : (2 * t + 1) * LANE] = even
            out[:, (2 * t + 1) * LANE : (2 * t + 2) * LANE] = odd


def matrices_from_rows(rows, out):
    count = out.shape[0]

    def body(m, carry):
        out[m] = rows[pl.ds(m, NB, stride=count), :]
        return carry

    lax.fori_loop(0, count, body, 0, unroll=4)


def hamilton_kernel(h, out, rows):
    count = out.shape[0]
    for t in range(h.shape[2] // LANE):
        cols = slice(t * LANE, (t + 1) * LANE)
        even, odd = rows_of(h[0, :, cols], h[1, :, cols])
        rows[2 * t * count : (2 * t + 1) * count, :] = even
        rows[(2 * t + 1) * count : (2 * t + 2) * count, :] = odd
    matrices_from_rows(rows, out)


def state_kernel(place, *refs):
    pieces, out, rows = refs[:-2], refs[-2], refs[-1]
    j = place[1]
    count = out.shape[0]
    own = pieces[0].shape[1] // LANE
    for k, piece in enumerate(pieces):
        for a in range(own):
            at = pl.multiple_of(((j ^ k) * own + a) * count, count)
            rows[pl.ds(at, count), :] = piece[:, a * LANE : (a + 1) * LANE]
    matrices_from_rows(rows, out)


def coupling_kernel(total, place, donors, counts, coupling, out):
    for t in range(coupling.shape[0]):
        for o in range(2 * REACH + 1):
            block = jnp.zeros((TILE, TILE), f32)
            for s in range(ND):
                shift = lax.rem(donors[t, s] - (place[2] + t) + REACH + total, total)
                used = jnp.logical_and(shift == o, s < counts[t])
                block = block - coupling[t, s].astype(f32) * jnp.where(used, 1.0, 0.0)
            out[t, :, o * TILE : (o + 1) * TILE] = block.astype(bf16)


def field(place, window, dense, dense_other, codes, outs, chunks):
    x, j = place[0], place[1]
    tiles = dense.shape[0]
    width = window.shape[1]
    ways = len(outs) // chunks
    g = x * (ways // 2) + j
    for t in range(2 * tiles):
        own = (t // tiles) == x
        weights = jnp.where(own, dense[t % tiles], dense_other[t % tiles])
        sigma = jnp.dot(weights, window[t * TILE : t * TILE + SPAN, :], preferred_element_type=f32)
        peak = jnp.max(jnp.abs(sigma), axis=1, keepdims=True)
        (code,), power = encode([sigma], peak)
        at = slice(t * TILE, (t + 1) * TILE)
        codes[at, :width] = code
        codes[at, width:] = jnp.broadcast_to(power, (TILE, LANE)).astype(i32).astype(i16)
    count = outs[0].shape[0]
    for c in range(chunks):
        for k in range(ways):
            at = pl.multiple_of(((g ^ k) * chunks + c) * count, count)
            outs[c * ways + k][...] = codes[pl.ds(at, count), :]


def field_one_kernel(chunks, place, mine, swap, straight, diag, dense, dense_other, *refs):
    outs, window, codes = refs[:-2], refs[-2], refs[-1]
    x = place[0]
    size = mine.shape[0]
    for ref, spot in ((mine, 1 + x), (swap, 2 - x), (straight, 3 - 3 * x), (diag, 3 * x)):
        window[pl.ds(pl.multiple_of(spot * size, size), size), :] = ref[...]
    field(place, window, dense, dense_other, codes, outs, chunks)


def field_two_kernel(chunks, place, dense, dense_other, *refs):
    states, outs, window, codes = refs[: 4 * chunks], refs[4 * chunks : -2], refs[-2], refs[-1]
    x, j = place[0], place[1]
    ways = len(outs) // chunks // 2
    for c in range(chunks):
        own, partner, near, far = states[4 * c : 4 * c + 4]
        count = own.shape[0] // ways
        for ref, spot in ((own, 1 + x), (partner, 2 - x), (near, 3 - 3 * x), (far, 3 * x)):
            for k in range(ways):
                at = ((spot * ways + (j ^ k)) * chunks + c) * count
                window[pl.ds(pl.multiple_of(at, count), count), :] = ref[k * count : (k + 1) * count, :]
    field(place, window, dense, dense_other, codes, outs, chunks)


def turned(rows):
    sign = jnp.where(half_lanes(rows.shape), 1.0, -1.0)
    return pltpu.roll(rows, NB, 1) * sign


def two_parts(values):
    high = values.astype(bf16)
    return high, (values - high.astype(f32)).astype(bf16)


def rate(h, s):
    h_high, h_low = two_parts(h)
    s_high, s_low = two_parts(s)
    ht_high, ht_low = two_parts(turned(h))
    st_high, st_low = two_parts(turned(s))
    left = jnp.concatenate(
        [jnp.concatenate([h_high, -s_high], 1), jnp.concatenate([h_low, -s_low], 1)], 0
    )
    right = jnp.concatenate(
        [
            jnp.concatenate([st_high, st_low], 1),
            jnp.concatenate([s_high, s_low], 1),
            jnp.concatenate([ht_high, ht_low], 1),
            jnp.concatenate([h_high, h_low], 1),
        ],
        0,
    )
    o = jnp.dot(left, right, preferred_element_type=f32)
    return (o[:NB, :LANE] + o[NB:, :LANE]) + (o[:NB, LANE:] + o[NB:, LANE:])


def unpack_field(place, pieces, rows):
    x, j = place[0], place[1]
    ways = len(pieces)
    g = x * (ways // 2) + j
    count = pieces[0].shape[0]
    own = pieces[0].shape[1] // LANE - 1
    for k, piece in enumerate(pieces):
        source = g ^ k
        first = ((source % (ways // 2)) * 2 + source // (ways // 2)) * own
        scale = decode_scale(piece[:, own * LANE :])
        for a in range(own):
            at = pl.multiple_of((first + a) * count, count)
            rows[pl.ds(at, count), :] = piece[:, a * LANE : (a + 1) * LANE].astype(i32).astype(f32) * scale


def first_kernel(place, h, s, *refs):
    ways = (len(refs) - 3) // 2
    pieces, middle, outs, rows, back = refs[:ways], refs[ways], refs[ways + 1 : -2], refs[-2], refs[-1]
    x, j = place[0], place[1]
    g = x * (ways // 2) + j
    count = middle.shape[0]
    unpack_field(place, pieces, rows)

    def body(m, carry):
        state = s[m]
        value = state + 0.5 * step_size * rate(h[m] + rows[pl.ds(m, NB, stride=count), :], state)
        middle[m] = value
        back[pl.ds(m, NB, stride=count), :] = value
        return carry

    lax.fori_loop(0, count, body, 0, unroll=4)
    own = outs[0].shape[1] // LANE
    for k, out in enumerate(outs):
        target = g ^ k
        first = ((target % (ways // 2)) * 2 + target // (ways // 2)) * own
        for a in range(own):
            at = pl.multiple_of((first + a) * count, count)
            out[:, a * LANE : (a + 1) * LANE] = back[pl.ds(at, count), :].astype(bf16)


def second_kernel(place, h, s, *refs):
    outs_n = (len(refs) - 2) // 3
    ways = 2 * outs_n
    pieces, outs, rows, back = refs[:ways], refs[ways:-2], refs[-2], refs[-1]
    j = place[1]
    count = outs[0].shape[0]
    unpack_field(place, pieces, rows)

    def body(m, carry):
        back[pl.ds(m, NB, stride=count), :] = rate(h[m] + rows[pl.ds(m, NB, stride=count), :], s[m])
        return carry

    lax.fori_loop(0, count, body, 0, unroll=4)
    own = outs[0].shape[1] // LANE - 1
    for k, out in enumerate(outs):
        first = (j ^ k) * own
        values = [back[pl.ds(pl.multiple_of((first + a) * count, count), count), :] for a in range(own)]
        peak = functools.reduce(jnp.maximum, [jnp.abs(v) for v in values])
        peak = jnp.max(peak, axis=1, keepdims=True)
        codes, power = encode(values, peak)
        for a in range(own):
            out[:, a * LANE : (a + 1) * LANE] = codes[a]
        out[:, own * LANE :] = jnp.broadcast_to(power, (count, LANE)).astype(i32).astype(i16)


def last_kernel(chunks, place, density, *refs):
    pieces, out = refs[:-1], refs[-1]
    j = place[1]
    ways = len(pieces) // chunks
    count = pieces[0].shape[0]
    own = pieces[0].shape[1] // LANE - 1
    for c in range(chunks):
        for k in range(ways):
            piece = pieces[c * ways + k]
            at = pl.ds(pl.multiple_of(((j ^ k) * chunks + c) * count, count), count)
            scale = decode_scale(piece[:, own * LANE :]) * step_size
            for t in range(own // 2):
                even = piece[:, 2 * t * LANE : (2 * t + 1) * LANE].astype(i32).astype(f32) * scale
                odd = piece[:, (2 * t + 1) * LANE : (2 * t + 2) * LANE].astype(i32).astype(f32) * scale
                real, imag = parts_of(even, odd)
                cols = slice(t * LANE, (t + 1) * LANE)
                out[0, at, cols] = density[0, at, cols] + real
                out[1, at, cols] = density[1, at, cols] + imag


def join_kernel(*refs):
    pieces, out = refs[:-1], refs[-1]
    count = pieces[0].shape[0]
    for k, piece in enumerate(pieces):
        out[k * count : (k + 1) * count, :] = piece[...]


def local(density, h_bands, coupling, donors, counts):
    nka, nb = lax.axis_size("ka"), lax.axis_size("ba")
    ways = 2 * nb
    i, j = lax.axis_index("ka"), lax.axis_index("ba")
    tiles, mom, pairs = coupling.shape[0], density.shape[1], density.shape[2]
    assert mom == tiles * TILE == REACH * TILE and nka % 2 == 0
    own = pairs // NB
    half = own // 2
    band = mom // nb
    chunks = 2 if band % 32 == 0 else 1
    count = band // chunks
    place = jnp.stack([i % 2, j, i * tiles]).astype(i32)

    def move(value, target):
        pairs_of = []
        for a in range(nka):
            for b in range(nb):
                ta, tb = target(a, b)
                pairs_of.append((a * nb + b, (ta % nka) * nb + tb))
        return lax.ppermute(value, ("ka", "ba"), pairs_of)

    def in_group(value, k):
        def target(a, b):
            t = ((a % 2) * nb + b) ^ k
            return a - a % 2 + t // nb, t % nb
        return value if k == 0 else move(value, target)

    def across(value):
        return move(value, lambda a, b: (a ^ 1, b))

    def along(value, odd, even):
        return move(value, lambda a, b: (a + (odd if a % 2 else even), b))

    shape = jax.ShapeDtypeStruct
    mine, other = call(round_kernel, [shape((mom, half * LANE), bf16)] * 2, n_in=1)(place, density)
    straight = along(mine, 2, -2)
    diag = along(other, 1, -1)
    swap = across(other)
    dense = call(
        functools.partial(coupling_kernel, nka * tiles),
        shape((tiles, TILE, SPAN), bf16),
        specs=[SMEM, SMEM, SMEM, VMEM],
    )(place, donors, counts, coupling)
    dense_other = across(dense)
    sent = call(split_kernel, [shape((band, own * LANE), f32)] * nb, n_in=1)(place, density)
    states = [in_group(v, k) for k, v in enumerate(sent)]
    matrices = shape((band, NB, LANE), f32)
    rows = pltpu.VMEM((band * NB, LANE), f32)
    state = call(state_kernel, matrices, [rows], n_in=nb)(place, *states)
    hamilton = call(hamilton_kernel, matrices, [rows], specs=[VMEM])(h_bands)

    window = pltpu.VMEM((4 * mom, half * LANE), bf16)
    codes = pltpu.VMEM((2 * mom, half * LANE + LANE), i16)
    pieces = [shape((count, half * LANE + LANE), i16)] * (ways * chunks)
    chunk_rows = pltpu.VMEM((count * NB, LANE), f32)
    chunk_shape = shape((count, NB, LANE), f32)

    fields = call(
        functools.partial(field_one_kernel, chunks), pieces, [window, codes], n_in=6
    )(place, mine, swap, straight, diag, dense, dense_other)

    middles, parts = [], []
    for c in range(chunks):
        got = [in_group(fields[c * ways + k], k) for k in range(ways)]
        at = slice(c * count, (c + 1) * count)
        middle, *outs = call(
            first_kernel,
            [chunk_shape] + [shape((count, half * LANE), bf16)] * ways,
            [chunk_rows, chunk_rows],
            n_in=2 + ways,
        )(place, hamilton[at], state[at], *got)
        middles.append(middle)
        back = [in_group(v, k) for k, v in enumerate(outs)]
        joined = shape((nb * count, half * LANE), bf16)
        own_part = call(join_kernel, joined, specs=[VMEM] * nb)(*back[:nb])
        partner = call(join_kernel, joined, specs=[VMEM] * nb)(*back[nb:])
        parts += [own_part, partner, along(own_part, 2, -2), along(partner, -2, 2)]

    fields = call(
        functools.partial(field_two_kernel, chunks), pieces, [window, codes], n_in=2 + 4 * chunks
    )(place, dense, dense_other, *parts)

    rates = []
    for c in range(chunks):
        got = [in_group(fields[c * ways + k], k) for k in range(ways)]
        outs = call(
            second_kernel,
            [shape((count, own * LANE + LANE), i16)] * nb,
            [chunk_rows, chunk_rows],
            n_in=2 + ways,
        )(place, hamilton[c * count : (c + 1) * count], middles[c], *got)
        rates += [in_group(v, k) for k, v in enumerate(outs)]
    return call(
        functools.partial(last_kernel, chunks), shape(density.shape, f32), n_in=1 + nb * chunks
    )(place, density, *rates)


def solution(mesh):
    placed = (
        P(None, "ka", "ba"),
        P(None, ("ka", "ba"), None),
        P("ka", None, None, None),
        P("ka", None),
        P("ka"),
    )
    return jax.shard_map(
        local, mesh=mesh, in_specs=placed, out_specs=P(None, "ka", "ba"), check_vma=False
    )
```

```python
import functools
ACUTS = 2
ECUTS = 2

import jax
import jax.numpy as jnp
from jax import lax
from jax.experimental import pallas as pl
from jax.experimental.pallas import tpu as pltpu
from jax.sharding import PartitionSpec as P

NB = 64
TILE = 128
ND = 4
REACH = 2
LANE = 2 * NB
SPAN = (2 * REACH + 1) * TILE
PACK = 16

step_size = 0.25
f32, bf16, i16, i32 = jnp.float32, jnp.bfloat16, jnp.int16, jnp.int32
SMEM = pl.BlockSpec(memory_space=pltpu.SMEM)
VMEM = pl.BlockSpec(memory_space=pltpu.VMEM)


def call(kernel, out, scratch=(), specs=None, n_in=0, work=1.0):
    return pl.pallas_call(
        kernel,
        out_shape=out,
        in_specs=specs if specs is not None else [SMEM] + [VMEM] * n_in,
        scratch_shapes=scratch,
        compiler_params=pltpu.CompilerParams(vmem_limit_bytes=48 * 2**20),
        cost_estimate=pl.CostEstimate(flops=0, bytes_accessed=int(work * 3.6e6), transcendentals=0),
    )


def half_lanes(shape):
    return lax.broadcasted_iota(i32, shape, 1) < NB


def rows_of(real, imag):
    low = half_lanes(real.shape)
    even = jnp.where(low, real, pltpu.roll(imag, NB, 1))
    odd = jnp.where(low, pltpu.roll(real, NB, 1), imag)
    return even, odd


def parts_of(even, odd):
    low = half_lanes(even.shape)
    real = jnp.where(low, even, pltpu.roll(odd, NB, 1))
    imag = jnp.where(low, pltpu.roll(even, NB, 1), odd)
    return real, imag


def encode(values, peak):
    power = jnp.ceil(jnp.log2(jnp.maximum(peak, 1e-30)))
    scale = jnp.exp2(15.0 - power)
    codes = [jnp.clip(jnp.round(v * scale), -32767.0, 32767.0).astype(i32).astype(i16) for v in values]
    return codes, power


def own_lane(shape):
    return lax.broadcasted_iota(i32, shape, 0) == lax.broadcasted_iota(i32, shape, 1)


def put_power(out, at, power):
    wide = jnp.where(own_lane((power.shape[0], LANE)), power, 0.0)
    line = jnp.sum(wide, axis=0, keepdims=True)
    out[at : at + PACK, :] = jnp.broadcast_to(line, (PACK, LANE)).astype(i32).astype(i16)


def get_scale(piece, at, count):
    line = piece[at : at + PACK, :].astype(i32).astype(f32)[:1]
    wide = jnp.where(own_lane((count, LANE)), jnp.broadcast_to(line, (count, LANE)), 0.0)
    return jnp.broadcast_to(jnp.exp2(jnp.sum(wide, axis=1, keepdims=True) - 15.0), (count, LANE))


def round_kernel(density, *outs):
    width = density.shape[2] // len(outs)
    for n, out in enumerate(outs):
        for t in range(width // LANE):
            cols = slice(n * width + t * LANE, n * width + (t + 1) * LANE)
            even, odd = rows_of(density[0, :, cols], density[1, :, cols])
            out[:, 2 * t * LANE : (2 * t + 1) * LANE] = even.astype(bf16)
            out[:, (2 * t + 1) * LANE : (2 * t + 2) * LANE] = odd.astype(bf16)


def split_kernel(place, density, *outs):
    j = place[1]
    rows = outs[0].shape[0]
    for k, out in enumerate(outs):
        at = pl.ds(pl.multiple_of((j ^ k) * rows, rows), rows)
        for t in range(density.shape[2] // LANE):
            cols = slice(t * LANE, (t + 1) * LANE)
            even, odd = rows_of(density[0, at, cols], density[1, at, cols])
            out[:, 2 * t * LANE : (2 * t + 1) * LANE] = even
            out[:, (2 * t + 1) * LANE : (2 * t + 2) * LANE] = odd


def step_of(count):
    return count + 8


def matrices_from_rows(rows, out):
    count = out.shape[0]

    def body(m, carry):
        out[m] = rows[pl.ds(m, NB, stride=step_of(count)), :]
        return carry

    lax.fori_loop(0, count, body, 0, unroll=8)


def hamilton_kernel(h, out, rows):
    count = out.shape[0]
    for t in range(h.shape[2] // LANE):
        cols = slice(t * LANE, (t + 1) * LANE)
        even, odd = rows_of(h[0, :, cols], h[1, :, cols])
        for a, value in ((2 * t, even), (2 * t + 1, odd)):
            rows[a * step_of(count) : a * step_of(count) + count, :] = value
    matrices_from_rows(rows, out)


def state_kernel(place, *refs):
    pieces, out, rows = refs[:-2], refs[-2], refs[-1]
    j = place[1]
    count = out.shape[0]
    own = pieces[0].shape[1] // LANE
    for k, piece in enumerate(pieces):
        for a in range(own):
            at = pl.multiple_of(((j ^ k) * own + a) * step_of(count), 8)
            rows[pl.ds(at, count), :] = piece[:, a * LANE : (a + 1) * LANE]
    matrices_from_rows(rows, out)


def coupling_kernel(total, place, donors, counts, coupling, out):
    tiles = coupling.shape[0]
    blocks = {}
    for t in range(tiles):
        for o in range(2 * REACH + 1):
            block = jnp.zeros((TILE, TILE), f32)
            for s in range(ND):
                shift = lax.rem(donors[t, s] - (place[2] + t) + REACH + total, total)
                used = jnp.logical_and(shift == o, s < counts[t])
                block = block - coupling[t, s].astype(f32) * jnp.where(used, 1.0, 0.0)
            blocks[t, t + o] = block.astype(bf16)
    empty = jnp.zeros((TILE, TILE), bf16)
    for t in range(tiles):
        for n in range(3 * tiles):
            mirror = (2 - n // tiles) * tiles + n % tiles
            value = jnp.where(place[0] == 1, blocks.get((t, n), empty), blocks.get((t, mirror), empty))
            out[t * TILE : (t + 1) * TILE, n * TILE : (n + 1) * TILE] = value


def field(place, weights, states, codes, powers, outs, chunks):
    j = place[1]
    ways = len(outs) // chunks
    sigma = jnp.dot(weights, states, preferred_element_type=f32)
    (code,), power = encode([sigma], jnp.max(jnp.abs(sigma), axis=1, keepdims=True))
    codes[...] = code
    powers[...] = jnp.broadcast_to(power, powers.shape)
    blocks = codes.shape[1] // LANE
    count = (outs[0].shape[0] - PACK) // blocks
    for c in range(chunks):
        for k in range(ways):
            at = pl.ds(pl.multiple_of(((j ^ k) * chunks + c) * count, count), count)
            out = outs[c * ways + k]
            for a in range(blocks):
                out[a * count : (a + 1) * count, :] = codes[at, a * LANE : (a + 1) * LANE]
            put_power(out, blocks * count, powers[at, :1])


def field_one_kernel(place, dense, mine, swap, passed, *refs):
    outs, (codes, powers) = refs[:-2], refs[-2:]
    states = jnp.concatenate([swap[...], mine[...], passed[...]], 0)
    field(place, dense[...], states, codes, powers, outs, 1)


def field_two_kernel(chunks, cuts, place, dense, *refs):
    n = 3 * chunks * cuts
    states, outs, (codes, powers, window) = refs[:n], refs[n:-3], refs[-3:]
    j = place[1]
    ways = len(outs) // chunks
    for c in range(chunks):
        for q in range(cuts):
            for b in range(3):
                ref = states[(c * cuts + q) * 3 + b]
                count, width = ref.shape[0] // ways, ref.shape[1]
                for k in range(ways):
                    at = ((b * ways + (j ^ k)) * chunks + c) * count
                    window[pl.ds(pl.multiple_of(at, count), count), q * width : (q + 1) * width] = ref[
                        k * count : (k + 1) * count, :
                    ]
    field(place, dense[...], window[...], codes, powers, outs, chunks)


def two_parts(values):
    high = values.astype(bf16)
    return high, (values - high.astype(f32)).astype(bf16)


def turned(rows):
    moved = pltpu.roll(rows, NB, 1)
    return jnp.where(half_lanes(rows.shape), moved, -moved)


def rate(h, s):
    h_high, h_low = two_parts(h)
    s_high, s_low = two_parts(s)
    left = jnp.concatenate(
        [jnp.concatenate([h_high, -s_high], 1), jnp.concatenate([h_low, -s_low], 1)], 0
    )
    right = [
        jnp.concatenate([turned(sp), sp, turned(hp), hp], 0) for sp, hp in ((s_high, h_high), (s_low, h_low))
    ]
    o = jnp.dot(left, jnp.concatenate(right, 1), preferred_element_type=f32)
    return (o[:NB, :LANE] + o[NB:, :LANE]) + (o[:NB, LANE:] + o[NB:, LANE:])


def unpack_field(place, cuts, count, first_row, pieces, rows):
    j = place[1]
    ways = len(pieces) // cuts
    whole = pieces[0].shape[0] - PACK
    own = NB // cuts // ways
    stride = whole // own
    for q in range(cuts):
        for k in range(ways):
            piece = pieces[q * ways + k]
            first = ((j ^ k) * cuts + q) * own
            scale = get_scale(piece, whole, stride)[first_row : first_row + count]
            for a in range(own):
                at = pl.multiple_of((first + a) * step_of(count), 8)
                code = piece[a * stride + first_row : a * stride + first_row + count, :]
                rows[pl.ds(at, count), :] = code.astype(i32).astype(f32) * scale


def first_kernel(cuts, n, first_row, place, h, s, *refs):
    pieces, middle, outs, rows, back = refs[:n], refs[n], refs[n + 1 : -2], refs[-2], refs[-1]
    j = place[1]
    count = middle.shape[0]
    step = step_of(count)
    unpack_field(place, cuts, count, first_row, pieces, rows)

    def body(m, carry):
        state = s[m]
        value = state + 0.5 * step_size * rate(h[m] + rows[pl.ds(m, NB, stride=step), :], state)
        middle[m] = value
        back[pl.ds(m, NB, stride=step), :] = value
        return carry

    lax.fori_loop(0, count, body, 0, unroll=16)
    own = outs[0].shape[1] // LANE
    for k, out in enumerate(outs):
        for a in range(own):
            at = pl.multiple_of(((j ^ k) * own + a) * step, 8)
            out[:, a * LANE : (a + 1) * LANE] = back[pl.ds(at, count), :].astype(bf16)


def second_kernel(ways, place, h, s, *refs):
    pieces, outs, rows, back = refs[:ways], refs[ways:-2], refs[-2], refs[-1]
    j = place[1]
    count = h.shape[0]
    step = step_of(count)
    unpack_field(place, 1, count, 0, pieces, rows)

    def body(m, carry):
        back[pl.ds(m, NB, stride=step), :] = rate(h[m] + rows[pl.ds(m, NB, stride=step), :], s[m])
        return carry

    lax.fori_loop(0, count, body, 0, unroll=16)
    own = (outs[0].shape[0] - PACK) // count
    for k, out in enumerate(outs):
        first = (j ^ k) * own
        values = [back[pl.ds(pl.multiple_of((first + a) * step, 8), count), :] for a in range(own)]
        peak = functools.reduce(jnp.maximum, [jnp.abs(v) for v in values])
        codes, power = encode(values, jnp.max(peak, axis=1, keepdims=True))
        for a in range(own):
            out[a * count : (a + 1) * count, :] = codes[a]
        put_power(out, own * count, power)


def last_kernel(chunks, place, density, *refs):
    pieces, out = refs[:-1], refs[-1]
    j = place[1]
    ways = len(pieces) // chunks
    own = 2 * density.shape[2] // LANE
    count = (pieces[0].shape[0] - PACK) // own
    for c in range(chunks):
        for k in range(ways):
            piece = pieces[c * ways + k]
            at = pl.ds(pl.multiple_of(((j ^ k) * chunks + c) * count, count), count)
            scale = get_scale(piece, own * count, count) * step_size
            block = lambda a: piece[a * count : (a + 1) * count, :].astype(i32).astype(f32) * scale
            for t in range(own // 2):
                real, imag = parts_of(block(2 * t), block(2 * t + 1))
                cols = slice(t * LANE, (t + 1) * LANE)
                out[0, at, cols] = density[0, at, cols] + real
                out[1, at, cols] = density[1, at, cols] + imag


def join_kernel(cuts, *refs):
    pieces, outs = refs[:-cuts], refs[-cuts:]
    count, width = pieces[0].shape[0], outs[0].shape[1]
    for q, out in enumerate(outs):
        for k, piece in enumerate(pieces):
            out[k * count : (k + 1) * count, :] = piece[:, q * width : (q + 1) * width]


def tie(values, *others):
    return lax.optimization_barrier((values, others))[0]


def local(density, h_bands, coupling, donors, counts):
    nka, nb = lax.axis_size("ka"), lax.axis_size("ba")
    i, j = lax.axis_index("ka"), lax.axis_index("ba")
    tiles, mom, pairs = coupling.shape[0], density.shape[1], density.shape[2]
    assert mom == tiles * TILE == REACH * TILE and nka % 2 == 0
    own = pairs // NB
    band = mom // nb
    chunks = 2 if band % 32 == 0 else 1
    count = band // chunks
    place = jnp.stack([i % 2, j, i * tiles]).astype(i32)

    def move(value, target):
        pairs_of = []
        for a in range(nka):
            for b in range(nb):
                ta, tb = target(a, b)
                pairs_of.append((a * nb + b, (ta % nka) * nb + tb))
        return lax.ppermute(value, ("ka", "ba"), pairs_of)

    def in_group(value, k):
        return value if k == 0 else move(value, lambda a, b: (a, b ^ k))

    def across(value):
        return move(value, lambda a, b: (a ^ 1, b))

    def onward(value):
        return move(value, lambda a, b: (a - 2 if a % 2 else a + 2, b))

    shape = jax.ShapeDtypeStruct
    cuts = max(n for n in (1, 2, 4) if n <= ACUTS and own % (2 * n) == 0)
    ecuts = max(n for n in (1, 2, 4) if n <= ECUTS and own % (2 * n) == 0)
    part = own // cuts
    mine = call(round_kernel, [shape((mom, part * LANE), bf16)] * cuts, specs=[VMEM])(density)
    swap = [across(v) for v in mine]
    passed = [onward(v) for v in swap]
    dense = call(
        functools.partial(coupling_kernel, nka * tiles),
        shape((mom, 3 * mom), bf16),
        specs=[SMEM, SMEM, SMEM, VMEM],
    )(place, donors, counts, coupling)
    sent = call(split_kernel, [shape((band, own * LANE), f32)] * nb, n_in=1)(place, density)
    states = [in_group(v, k) for k, v in enumerate(sent)]
    matrices = shape((band, NB, LANE), f32)
    rows = pltpu.VMEM((step_of(band) * NB, LANE), f32)
    hamilton = call(hamilton_kernel, matrices, [rows], specs=[VMEM])(h_bands)
    hamilton, passed[0] = lax.optimization_barrier((hamilton, passed[0]))

    got, fields = [], []
    for q in range(cuts):
        fields = call(
            field_one_kernel,
            [shape((part * band + PACK, LANE), i16)] * nb,
            [pltpu.VMEM((mom, part * LANE), i16), pltpu.VMEM((mom, LANE), f32)],
            n_in=4,
        )(place, dense, mine[q], swap[q], passed[q])
        got += [in_group(v, k) for k, v in enumerate(fields)]
    state = call(state_kernel, matrices, [rows], n_in=nb)(place, *states)

    chunk_rows = pltpu.VMEM((step_of(count) * NB, LANE), f32)
    chunk_shape = shape((count, NB, LANE), f32)
    middles, parts = [], []
    for c in range(chunks):
        at = slice(c * count, (c + 1) * count)
        hc, sc = hamilton[at], state[at]
        middle, *outs = call(
            functools.partial(first_kernel, cuts, nb * cuts, c * count),
            [chunk_shape] + [shape((count, own * LANE), bf16)] * nb,
            [chunk_rows, chunk_rows],
            n_in=2 + nb * cuts,
        )(place, hc, sc, *got)
        middles.append(middle)
        back = [in_group(v, k) for k, v in enumerate(outs)]
        joined = [shape((nb * count, own // ecuts * LANE), bf16)] * ecuts
        mine = call(functools.partial(join_kernel, ecuts), joined, specs=[VMEM] * nb)(*back)
        for q in range(ecuts):
            swap = across(mine[q])
            parts += [swap, mine[q], onward(swap)]

    fields = call(
        functools.partial(field_two_kernel, chunks, ecuts),
        [shape((own * count + PACK, LANE), i16)] * (nb * chunks),
        [pltpu.VMEM((mom, own * LANE), i16), pltpu.VMEM((mom, LANE), f32), pltpu.VMEM((3 * mom, own * LANE), bf16)],
        n_in=1 + len(parts),
    )(place, dense, *parts)
    got = [[in_group(fields[c * nb + k], k) for k in range(nb)] for c in range(chunks)]
    rates = []
    for c in range(chunks):
        hc, sc = hamilton[c * count : (c + 1) * count], middles[c]
        outs = call(
            functools.partial(second_kernel, nb),
            [shape((own * count + PACK, LANE), i16)] * nb,
            [chunk_rows, chunk_rows],
            n_in=2 + nb,
        )(place, hc, sc, *got[c])
        rates += [in_group(v, k) for k, v in enumerate(outs)]
    return call(
        functools.partial(last_kernel, chunks), shape(density.shape, f32), n_in=1 + nb * chunks
    )(place, density, *rates)


def solution(mesh):
    placed = (
        P(None, "ka", "ba"),
        P(None, ("ka", "ba"), None),
        P("ka", None, None, None),
        P("ka", None),
        P("ka"),
    )
    return jax.shard_map(
        local, mesh=mesh, in_specs=placed, out_specs=P(None, "ka", "ba"), check_vma=False
    )
```

```python
import functools
CUTS = 3

import jax
import jax.numpy as jnp
from jax import lax
from jax.experimental import pallas as pl
from jax.experimental.pallas import tpu as pltpu
from jax.sharding import PartitionSpec as P

NB = 64
TILE = 128
ND = 4
REACH = 2
LANE = 2 * NB
SPAN = (2 * REACH + 1) * TILE
PACK = 16

step_size = 0.25
f32, bf16, i16, i32 = jnp.float32, jnp.bfloat16, jnp.int16, jnp.int32
SMEM = pl.BlockSpec(memory_space=pltpu.SMEM)
VMEM = pl.BlockSpec(memory_space=pltpu.VMEM)


def call(kernel, out, scratch=(), specs=None, n_in=0, work=1.0):
    return pl.pallas_call(
        kernel,
        out_shape=out,
        in_specs=specs if specs is not None else [SMEM] + [VMEM] * n_in,
        scratch_shapes=scratch,
        compiler_params=pltpu.CompilerParams(vmem_limit_bytes=20 * 2**20),
        cost_estimate=pl.CostEstimate(flops=0, bytes_accessed=int(work * 3.6e6), transcendentals=0),
    )


def half_lanes(shape):
    return lax.broadcasted_iota(i32, shape, 1) < NB


def rows_of(real, imag):
    low = half_lanes(real.shape)
    crossed = pltpu.roll(jnp.where(low, imag, real), NB, 1)
    return jnp.where(low, real, crossed), jnp.where(low, crossed, imag)


def parts_of(even, odd):
    low = half_lanes(even.shape)
    crossed = pltpu.roll(jnp.where(low, odd, even), NB, 1)
    return jnp.where(low, even, crossed), jnp.where(low, crossed, odd)


def encode(values, peak):
    power = jnp.ceil(jnp.log2(jnp.maximum(peak, 1e-30)))
    scale = jnp.exp2(15.0 - power)
    codes = [jnp.clip(jnp.round(v * scale), -32767.0, 32767.0).astype(i32).astype(i16) for v in values]
    return codes, power


def own_lane(shape):
    return lax.broadcasted_iota(i32, shape, 0) == lax.broadcasted_iota(i32, shape, 1)


def put_power(out, at, power):
    wide = jnp.where(own_lane((power.shape[0], LANE)), power, 0.0)
    line = jnp.sum(wide, axis=0, keepdims=True)
    out[at : at + PACK, :] = jnp.broadcast_to(line, (PACK, LANE)).astype(i32).astype(i16)


def get_scale(piece, at, count):
    line = piece[at : at + PACK, :].astype(i32).astype(f32)[:1]
    wide = jnp.where(own_lane((count, LANE)), jnp.broadcast_to(line, (count, LANE)), 0.0)
    return jnp.broadcast_to(jnp.exp2(jnp.sum(wide, axis=1, keepdims=True) - 15.0), (count, LANE))


def round_kernel(density, *outs):
    at = 0
    for out in outs:
        for t in range(out.shape[1] // LANE // 2):
            cols = slice(at, at + LANE)
            at += LANE
            even, odd = rows_of(density[0, :, cols], density[1, :, cols])
            out[:, 2 * t * LANE : (2 * t + 1) * LANE] = even.astype(bf16)
            out[:, (2 * t + 1) * LANE : (2 * t + 2) * LANE] = odd.astype(bf16)


def split_kernel(place, density, *outs):
    j = place[1]
    rows = outs[0].shape[0]
    for k, out in enumerate(outs):
        at = pl.ds(pl.multiple_of((j ^ k) * rows, rows), rows)
        for t in range(density.shape[2] // LANE):
            cols = slice(t * LANE, (t + 1) * LANE)
            even, odd = rows_of(density[0, at, cols], density[1, at, cols])
            out[:, 2 * t * LANE : (2 * t + 1) * LANE] = even
            out[:, (2 * t + 1) * LANE : (2 * t + 2) * LANE] = odd


def step_of(count):
    return count + 8


def matrices_from_rows(rows, out):
    count = out.shape[0]

    def body(m, carry):
        out[m] = rows[pl.ds(m, NB, stride=step_of(count)), :]
        return carry

    lax.fori_loop(0, count, body, 0, unroll=8)


def hamilton_kernel(h, out, rows):
    count = out.shape[0]
    for t in range(h.shape[2] // LANE):
        cols = slice(t * LANE, (t + 1) * LANE)
        even, odd = rows_of(h[0, :, cols], h[1, :, cols])
        for a, value in ((2 * t, even), (2 * t + 1, odd)):
            rows[a * step_of(count) : a * step_of(count) + count, :] = value
    matrices_from_rows(rows, out)


def state_kernel(place, *refs):
    pieces, out, rows = refs[:-2], refs[-2], refs[-1]
    j = place[1]
    count = out.shape[0]
    own = pieces[0].shape[1] // LANE
    for k, piece in enumerate(pieces):
        for a in range(own):
            at = pl.multiple_of(((j ^ k) * own + a) * step_of(count), 8)
            rows[pl.ds(at, count), :] = piece[:, a * LANE : (a + 1) * LANE]
    matrices_from_rows(rows, out)


def coupling_kernel(total, place, donors, counts, coupling, out):
    tiles = coupling.shape[0]
    blocks = {}
    for t in range(tiles):
        for o in range(2 * REACH + 1):
            block = jnp.zeros((TILE, TILE), f32)
            for s in range(ND):
                shift = lax.rem(donors[t, s] - (place[2] + t) + REACH + total, total)
                used = jnp.logical_and(shift == o, s < counts[t])
                block = block - coupling[t, s].astype(f32) * jnp.where(used, 1.0, 0.0)
            blocks[t, t + o] = block.astype(bf16)
    empty = jnp.zeros((TILE, TILE), bf16)
    for t in range(tiles):
        for n in range(3 * tiles):
            mirror = (2 - n // tiles) * tiles + n % tiles
            value = jnp.where(place[0] == 1, blocks.get((t, n), empty), blocks.get((t, mirror), empty))
            out[t * TILE : (t + 1) * TILE, n * TILE : (n + 1) * TILE] = value


def field(place, weights, states, codes, powers, outs):
    j = place[1]
    sigma = jnp.dot(weights, states, preferred_element_type=f32)
    (code,), power = encode([sigma], jnp.max(jnp.abs(sigma), axis=1, keepdims=True))
    codes[...] = code
    powers[...] = jnp.broadcast_to(power, powers.shape)
    blocks = codes.shape[1] // LANE
    count = (outs[0].shape[0] - PACK) // blocks
    for k, out in enumerate(outs):
        at = pl.ds(pl.multiple_of((j ^ k) * count, count), count)
        for a in range(blocks):
            out[a * count : (a + 1) * count, :] = codes[at, a * LANE : (a + 1) * LANE]
        put_power(out, blocks * count, powers[at, :1])


def field_one_kernel(place, dense, mine, swap, passed, *refs):
    outs, (codes, powers) = refs[:-2], refs[-2:]
    states = jnp.concatenate([swap[...], mine[...], passed[...]], 0)
    field(place, dense[...], states, codes, powers, outs)


def rows_for(dense, ways, start, count):
    band = dense.shape[0] // ways
    return jnp.concatenate([dense[w * band + start : w * band + start + count, :] for w in range(ways)], 0)


def window_field_kernel(spots, start, place, dense, *refs):
    n = len(spots)
    states, outs, (window, codes, powers) = refs[:n], refs[n:-3], refs[-3:]
    j = place[1]
    ways = len(outs)
    band = window.shape[0] // 3 // ways
    for ref, (b, first, lane) in zip(states, spots):
        count, width = ref.shape[0] // ways, ref.shape[1]
        for k in range(ways):
            at = pl.multiple_of((b * ways + (j ^ k)) * band + first, PACK)
            window[pl.ds(at, count), lane : lane + width] = ref[k * count : (k + 1) * count, :]
    count = codes.shape[0] // ways
    field(place, rows_for(dense, ways, start, count), window[...], codes, powers, outs)


def field_kernel(start, place, dense, window, *refs):
    outs, (codes, powers) = refs[:-2], refs[-2:]
    count = codes.shape[0] // len(outs)
    field(place, rows_for(dense, len(outs), start, count), window[...], codes, powers, outs)


def two_parts(values):
    high = values.astype(bf16)
    return high, (values - high.astype(f32)).astype(bf16)


def turned(rows):
    moved = pltpu.roll(rows, NB, 1)
    return jnp.where(half_lanes(rows.shape), moved, -moved)


def rate(h, s):
    h_high, h_low = two_parts(h)
    s_high, s_low = two_parts(s)
    left = jnp.concatenate(
        [jnp.concatenate([h_high, -s_high], 1), jnp.concatenate([h_low, -s_low], 1)], 0
    )
    right = [
        jnp.concatenate([turned(sp), sp, turned(hp), hp], 0) for sp, hp in ((s_high, h_high), (s_low, h_low))
    ]
    o = jnp.dot(left, jnp.concatenate(right, 1), preferred_element_type=f32)
    return (o[:NB, :LANE] + o[NB:, :LANE]) + (o[:NB, LANE:] + o[NB:, LANE:])


def unpack_field(place, cuts, count, first_row, stride, pieces, rows):
    j = place[1]
    ways = len(pieces) // cuts
    offset = 0
    for q in range(cuts):
        whole = pieces[q * ways].shape[0] - PACK
        own = whole // stride
        for k in range(ways):
            piece = pieces[q * ways + k]
            first = (j ^ k) * (NB // ways) + offset
            scale = get_scale(piece, whole, stride)[first_row : first_row + count]
            for a in range(own):
                at = pl.multiple_of((first + a) * step_of(count), 8)
                code = piece[a * stride + first_row : a * stride + first_row + count, :]
                rows[pl.ds(at, count), :] = code.astype(i32).astype(f32) * scale
        offset += own


def first_kernel(cuts, n, first_row, band, place, h, s, *refs):
    pieces, middle, outs, rows, back = refs[:n], refs[n], refs[n + 1 : -2], refs[-2], refs[-1]
    j = place[1]
    count = middle.shape[0]
    step = step_of(count)
    unpack_field(place, cuts, count, first_row, band, pieces, rows)

    def body(m, carry):
        state = s[m]
        value = state + 0.5 * step_size * rate(h[m] + rows[pl.ds(m, NB, stride=step), :], state)
        middle[m] = value
        back[pl.ds(m, NB, stride=step), :] = value
        return carry

    lax.fori_loop(0, count, body, 0, unroll=16)
    own = outs[0].shape[1] // LANE
    for k, out in enumerate(outs):
        for a in range(own):
            at = pl.multiple_of(((j ^ k) * own + a) * step, 8)
            out[:, a * LANE : (a + 1) * LANE] = back[pl.ds(at, count), :].astype(bf16)


def second_kernel(ways, place, h, s, *refs):
    pieces, outs, rows, back = refs[:ways], refs[ways:-2], refs[-2], refs[-1]
    j = place[1]
    count = h.shape[0]
    step = step_of(count)
    unpack_field(place, 1, count, 0, count, pieces, rows)

    def body(m, carry):
        back[pl.ds(m, NB, stride=step), :] = rate(h[m] + rows[pl.ds(m, NB, stride=step), :], s[m])
        return carry

    lax.fori_loop(0, count, body, 0, unroll=16)
    own = (outs[0].shape[0] - PACK) // count
    for k, out in enumerate(outs):
        first = (j ^ k) * own
        values = [back[pl.ds(pl.multiple_of((first + a) * step, 8), count), :] for a in range(own)]
        peak = functools.reduce(jnp.maximum, [jnp.abs(v) for v in values])
        codes, power = encode(values, jnp.max(peak, axis=1, keepdims=True))
        for a in range(own):
            out[a * count : (a + 1) * count, :] = codes[a]
        put_power(out, own * count, power)


def last_kernel(chunks, place, *refs):
    states, pieces, (out, done, sems) = refs[: -3 - len(refs[:-3]) * chunks // (1 + chunks)], refs[:-3], refs[-3:]
    ways = len(states)
    pieces = pieces[ways:]
    j = place[1]
    own = states[0].shape[1] // LANE
    count = states[0].shape[0] // chunks
    copies = []
    for c in range(chunks):
        for k in range(ways):
            piece = pieces[c * ways + k]
            here = slice(c * count, (c + 1) * count)
            at = pl.ds(pl.multiple_of(((j ^ k) * chunks + c) * count, count), count)
            spot = (c * ways + k) * count
            scale = get_scale(piece, own * count, count) * step_size

            def block(a):
                code = piece[a * count : (a + 1) * count, :]
                return states[k][here, a * LANE : (a + 1) * LANE] + code.astype(i32).astype(f32) * scale

            for t in range(own // 2):
                real, imag = parts_of(block(2 * t), block(2 * t + 1))
                done[0, spot : spot + count, t * LANE : (t + 1) * LANE] = real
                done[1, spot : spot + count, t * LANE : (t + 1) * LANE] = imag
            copies.append(
                pltpu.make_async_copy(
                    done.at[:, spot : spot + count, :], out.at[:, at, :], sems.at[c * ways + k]
                )
            )
            copies[-1].start()
    for copy in copies:
        copy.wait()


def join_kernel(cuts, *refs):
    pieces, outs = refs[:-cuts], refs[-cuts:]
    count = pieces[0].shape[0]
    at = 0
    for out in outs:
        width = out.shape[1]
        for k, piece in enumerate(pieces):
            out[k * count : (k + 1) * count, :] = piece[:, at : at + width]
        at += width


def tie(values, *others):
    return lax.optimization_barrier((values, others))[0]


def split_rows(own, parts):
    parts = min(parts, own // 2)
    return [2 * ((own // 2 + parts - 1 - n) // parts) for n in range(parts)]


def local(density, h_bands, coupling, donors, counts):
    nka, nb = lax.axis_size("ka"), lax.axis_size("ba")
    i, j = lax.axis_index("ka"), lax.axis_index("ba")
    tiles, mom, pairs = coupling.shape[0], density.shape[1], density.shape[2]
    assert mom == tiles * TILE == REACH * TILE and nka % 2 == 0
    own = pairs // NB
    band = mom // nb
    chunks = 2 if band % 32 == 0 else 1
    count = band // chunks
    place = jnp.stack([i % 2, j, i * tiles]).astype(i32)

    def move(value, target):
        pairs_of = []
        for a in range(nka):
            for b in range(nb):
                ta, tb = target(a, b)
                pairs_of.append((a * nb + b, (ta % nka) * nb + tb))
        return lax.ppermute(value, ("ka", "ba"), pairs_of)

    def in_group(value, k):
        return value if k == 0 else move(value, lambda a, b: (a, b ^ k))

    def across(value):
        return move(value, lambda a, b: (a ^ 1, b))

    def onward(value):
        return move(value, lambda a, b: (a - 2 if a % 2 else a + 2, b))

    shape = jax.ShapeDtypeStruct
    widths = split_rows(own, CUTS)
    cuts = len(widths)
    ecuts = 2 if own % 4 == 0 else 1
    mine = call(round_kernel, [shape((mom, w * LANE), bf16) for w in widths], specs=[VMEM])(density)
    swap = [across(v) for v in mine]
    passed = []
    for q, value in enumerate(swap):
        if q > 1:
            value = tie(value, passed[q - 2])
        passed.append(onward(value))
    dense = call(
        functools.partial(coupling_kernel, nka * tiles),
        shape((mom, 3 * mom), bf16),
        specs=[SMEM, SMEM, SMEM, VMEM],
    )(place, donors, counts, coupling)
    sent = call(split_kernel, [shape((band, own * LANE), f32)] * nb, n_in=1)(place, density)
    states = [in_group(v, k) for k, v in enumerate(sent)]
    matrices = shape((band, NB, LANE), f32)
    rows = pltpu.VMEM((step_of(band) * NB, LANE), f32)
    hamilton = call(hamilton_kernel, matrices, [rows], specs=[VMEM])(h_bands)
    hamilton, passed[0] = lax.optimization_barrier((hamilton, passed[0]))

    if cuts > 2:
        passed[1] = tie(passed[1], states)
    got, fields = [], []
    for q in range(cuts):
        if q > 1:
            passed[q] = tie(passed[q], got[(q - 2) * nb : (q - 1) * nb])
        fields = call(
            field_one_kernel,
            [shape((widths[q] * band + PACK, LANE), i16)] * nb,
            [pltpu.VMEM((mom, widths[q] * LANE), i16), pltpu.VMEM((mom, LANE), f32)],
            n_in=4,
        )(place, dense, mine[q], swap[q], passed[q])
        got += [in_group(v, k) for k, v in enumerate(fields)]
    state = call(state_kernel, matrices, [rows], n_in=nb)(place, *states)

    chunk_rows = pltpu.VMEM((step_of(count) * NB, LANE), f32)
    chunk_shape = shape((count, NB, LANE), f32)
    middles, parts, spots = [], [], []
    for c in range(chunks):
        at = slice(c * count, (c + 1) * count)
        hc, sc = hamilton[at], state[at]
        middle, *outs = call(
            functools.partial(first_kernel, cuts, nb * cuts, c * count, band),
            [chunk_shape] + [shape((count, own * LANE), bf16)] * nb,
            [chunk_rows, chunk_rows],
            n_in=2 + nb * cuts,
        )(place, hc, sc, *got)
        middles.append(middle)
        back = [in_group(v, k) for k, v in enumerate(outs)]
        ewidths = [own // ecuts] * ecuts
        joined = [shape((nb * count, w * LANE), bf16) for w in ewidths]
        mine = call(functools.partial(join_kernel, len(ewidths)), joined, specs=[VMEM] * nb)(*back)
        for q in range(len(ewidths)):
            swap = across(mine[q])
            parts += [swap, mine[q], onward(swap)]
            spots += [(b, c * count, sum(ewidths[:q]) * LANE) for b in range(3)]

    pieces = [shape((own * count + PACK, LANE), i16)] * nb
    room = [pltpu.VMEM((nb * count, own * LANE), i16), pltpu.VMEM((nb * count, LANE), f32)]
    *fields, window = call(
        functools.partial(window_field_kernel, spots, 0),
        pieces + [shape((3 * mom, own * LANE), bf16)],
        room,
        n_in=1 + len(parts),
    )(place, dense, *parts)
    for c in range(1, chunks):
        fields += call(functools.partial(field_kernel, c * count), pieces, room, n_in=2)(place, dense, window)
    got = [[in_group(fields[c * nb + k], k) for k in range(nb)] for c in range(chunks)]
    rates = []
    for c in range(chunks):
        hc, sc = hamilton[c * count : (c + 1) * count], middles[c]
        outs = call(
            functools.partial(second_kernel, nb),
            [shape((own * count + PACK, LANE), i16)] * nb,
            [chunk_rows, chunk_rows],
            n_in=2 + nb,
        )(place, hc, sc, *got[c])
        rates += [in_group(v, k) for k, v in enumerate(outs)]
    return pl.pallas_call(
        functools.partial(last_kernel, chunks),
        out_shape=shape(density.shape, f32),
        in_specs=[SMEM] + [VMEM] * (nb + nb * chunks),
        out_specs=pl.BlockSpec(memory_space=pl.ANY),
        scratch_shapes=[pltpu.VMEM(density.shape, f32), pltpu.SemaphoreType.DMA((nb * chunks,))],
        compiler_params=pltpu.CompilerParams(vmem_limit_bytes=20 * 2**20),
    )(place, *sent, *rates)


def solution(mesh):
    placed = (
        P(None, "ka", "ba"),
        P(None, ("ka", "ba"), None),
        P("ka", None, None, None),
        P("ka", None),
        P("ka"),
    )
    return jax.shard_map(
        local, mesh=mesh, in_specs=placed, out_specs=P(None, "ka", "ba"), check_vma=False
    )
```

```python
import functools
CUTS = 3

import jax
import jax.numpy as jnp
from jax import lax
from jax.experimental import pallas as pl
from jax.experimental.pallas import tpu as pltpu
from jax.sharding import PartitionSpec as P

NB = 64
TILE = 128
ND = 4
REACH = 2
LANE = 2 * NB
SPAN = (2 * REACH + 1) * TILE
PACK = 16

step_size = 0.25
f32, bf16, i16, i32 = jnp.float32, jnp.bfloat16, jnp.int16, jnp.int32
SMEM = pl.BlockSpec(memory_space=pltpu.SMEM)
VMEM = pl.BlockSpec(memory_space=pltpu.VMEM)


def call(kernel, out, scratch=(), specs=None, n_in=0, work=1.0):
    return pl.pallas_call(
        kernel,
        out_shape=out,
        in_specs=specs if specs is not None else [SMEM] + [VMEM] * n_in,
        scratch_shapes=scratch,
        compiler_params=pltpu.CompilerParams(vmem_limit_bytes=20 * 2**20),
        cost_estimate=pl.CostEstimate(flops=0, bytes_accessed=int(work * 3.6e6), transcendentals=0),
    )


def half_lanes(shape):
    return lax.broadcasted_iota(i32, shape, 1) < NB


def rows_of(real, imag):
    low = half_lanes(real.shape)
    crossed = pltpu.roll(jnp.where(low, imag, real), NB, 1)
    return jnp.where(low, real, crossed), jnp.where(low, crossed, imag)


def parts_of(even, odd):
    low = half_lanes(even.shape)
    crossed = pltpu.roll(jnp.where(low, odd, even), NB, 1)
    return jnp.where(low, even, crossed), jnp.where(low, crossed, odd)


def encode(values, peak):
    power = jnp.ceil(jnp.log2(jnp.maximum(peak, 1e-30)))
    scale = jnp.exp2(15.0 - power)
    codes = [jnp.clip(jnp.round(v * scale), -32767.0, 32767.0).astype(i32).astype(i16) for v in values]
    return codes, power


def own_lane(shape):
    return lax.broadcasted_iota(i32, shape, 0) == lax.broadcasted_iota(i32, shape, 1)


def put_power(out, at, power):
    wide = jnp.where(own_lane((power.shape[0], LANE)), power, 0.0)
    line = jnp.sum(wide, axis=0, keepdims=True)
    out[at : at + PACK, :] = jnp.broadcast_to(line, (PACK, LANE)).astype(i32).astype(i16)


def get_scale(piece, at, count):
    line = piece[at : at + PACK, :].astype(i32).astype(f32)[:1]
    wide = jnp.where(own_lane((count, LANE)), jnp.broadcast_to(line, (count, LANE)), 0.0)
    return jnp.broadcast_to(jnp.exp2(jnp.sum(wide, axis=1, keepdims=True) - 15.0), (count, LANE))


def round_kernel(density, *outs):
    at = 0
    for out in outs:
        for t in range(out.shape[1] // LANE // 2):
            cols = slice(at, at + LANE)
            at += LANE
            even, odd = rows_of(density[0, :, cols], density[1, :, cols])
            out[:, 2 * t * LANE : (2 * t + 1) * LANE] = even.astype(bf16)
            out[:, (2 * t + 1) * LANE : (2 * t + 2) * LANE] = odd.astype(bf16)


def split_kernel(place, density, *outs):
    j = place[1]
    rows = outs[0].shape[0]
    for k, out in enumerate(outs):
        at = pl.ds(pl.multiple_of((j ^ k) * rows, rows), rows)
        for t in range(density.shape[2] // LANE):
            cols = slice(t * LANE, (t + 1) * LANE)
            even, odd = rows_of(density[0, at, cols], density[1, at, cols])
            out[:, 2 * t * LANE : (2 * t + 1) * LANE] = even
            out[:, (2 * t + 1) * LANE : (2 * t + 2) * LANE] = odd


def step_of(count):
    return count + 8


def matrices_from_rows(rows, out):
    count = out.shape[0]

    def body(m, carry):
        out[m] = rows[pl.ds(m, NB, stride=step_of(count)), :]
        return carry

    lax.fori_loop(0, count, body, 0, unroll=8)


def hamilton_kernel(h, out, rows):
    count = out.shape[0]
    for t in range(h.shape[2] // LANE):
        cols = slice(t * LANE, (t + 1) * LANE)
        even, odd = rows_of(h[0, :, cols], h[1, :, cols])
        for a, value in ((2 * t, even), (2 * t + 1, odd)):
            rows[a * step_of(count) : a * step_of(count) + count, :] = value
    matrices_from_rows(rows, out)


def state_kernel(place, *refs):
    pieces, out, rows = refs[:-2], refs[-2], refs[-1]
    j = place[1]
    count = out.shape[0]
    own = pieces[0].shape[1] // LANE
    for k, piece in enumerate(pieces):
        for a in range(own):
            at = pl.multiple_of(((j ^ k) * own + a) * step_of(count), 8)
            rows[pl.ds(at, count), :] = piece[:, a * LANE : (a + 1) * LANE]
    matrices_from_rows(rows, out)


def coupling_kernel(total, place, donors, counts, coupling, out):
    tiles = coupling.shape[0]
    blocks = {}
    for t in range(tiles):
        for o in range(2 * REACH + 1):
            block = jnp.zeros((TILE, TILE), f32)
            for s in range(ND):
                shift = lax.rem(donors[t, s] - (place[2] + t) + REACH + total, total)
                used = jnp.logical_and(shift == o, s < counts[t])
                block = block - coupling[t, s].astype(f32) * jnp.where(used, 1.0, 0.0)
            blocks[t, t + o] = block.astype(bf16)
    empty = jnp.zeros((TILE, TILE), bf16)
    for t in range(tiles):
        for n in range(3 * tiles):
            mirror = (2 - n // tiles) * tiles + n % tiles
            value = jnp.where(place[0] == 1, blocks.get((t, n), empty), blocks.get((t, mirror), empty))
            out[t * TILE : (t + 1) * TILE, n * TILE : (n + 1) * TILE] = value


def field(place, weights, states, codes, powers, outs):
    j = place[1]
    sigma = jnp.dot(weights, states, preferred_element_type=f32)
    (code,), power = encode([sigma], jnp.max(jnp.abs(sigma), axis=1, keepdims=True))
    codes[...] = code
    powers[...] = jnp.broadcast_to(power, powers.shape)
    blocks = codes.shape[1] // LANE
    count = (outs[0].shape[0] - PACK) // blocks
    for k, out in enumerate(outs):
        at = pl.ds(pl.multiple_of((j ^ k) * count, count), count)
        for a in range(blocks):
            out[a * count : (a + 1) * count, :] = codes[at, a * LANE : (a + 1) * LANE]
        put_power(out, blocks * count, powers[at, :1])


def field_one_kernel(place, dense, mine, swap, passed, *refs):
    outs, (codes, powers) = refs[:-2], refs[-2:]
    states = jnp.concatenate([swap[...], mine[...], passed[...]], 0)
    field(place, dense[...], states, codes, powers, outs)


def rows_for(dense, ways, start, count):
    band = dense.shape[0] // ways
    return jnp.concatenate([dense[w * band + start : w * band + start + count, :] for w in range(ways)], 0)


def window_field_kernel(spots, start, place, dense, *refs):
    n = len(spots)
    states, outs, (window, codes, powers) = refs[:n], refs[n:-3], refs[-3:]
    j = place[1]
    ways = len(outs)
    band = window.shape[0] // 3 // ways
    for ref, (b, first, lane) in zip(states, spots):
        count, width = ref.shape[0] // ways, ref.shape[1]
        for k in range(ways):
            at = pl.multiple_of((b * ways + (j ^ k)) * band + first, PACK)
            window[pl.ds(at, count), lane : lane + width] = ref[k * count : (k + 1) * count, :]
    count = codes.shape[0] // ways
    field(place, rows_for(dense, ways, start, count), window[...], codes, powers, outs)


def field_kernel(start, place, dense, window, *refs):
    outs, (codes, powers) = refs[:-2], refs[-2:]
    count = codes.shape[0] // len(outs)
    field(place, rows_for(dense, len(outs), start, count), window[...], codes, powers, outs)


def two_parts(values):
    high = values.astype(bf16)
    return high, (values - high.astype(f32)).astype(bf16)


def turned(rows):
    moved = pltpu.roll(rows, NB, 1)
    return jnp.where(half_lanes(rows.shape), moved, -moved)


def rate(h, s):
    h_high, h_low = two_parts(h)
    s_high, s_low = two_parts(s)
    left = jnp.concatenate(
        [jnp.concatenate([h_high, -s_high], 1), jnp.concatenate([h_low, -s_low], 1)], 0
    )
    right = [
        jnp.concatenate([turned(sp), sp, turned(hp), hp], 0) for sp, hp in ((s_high, h_high), (s_low, h_low))
    ]
    o = jnp.dot(left, jnp.concatenate(right, 1), preferred_element_type=f32)
    return (o[:NB, :LANE] + o[NB:, :LANE]) + (o[:NB, LANE:] + o[NB:, LANE:])


def unpack_field(place, cuts, count, first_row, stride, pieces, rows):
    j = place[1]
    ways = len(pieces) // cuts
    offset = 0
    for q in range(cuts):
        whole = pieces[q * ways].shape[0] - PACK
        own = whole // stride
        for k in range(ways):
            piece = pieces[q * ways + k]
            first = (j ^ k) * (NB // ways) + offset
            scale = get_scale(piece, whole, stride)[first_row : first_row + count]
            for a in range(own):
                at = pl.multiple_of((first + a) * step_of(count), 8)
                code = piece[a * stride + first_row : a * stride + first_row + count, :]
                rows[pl.ds(at, count), :] = code.astype(i32).astype(f32) * scale
        offset += own


def first_kernel(cuts, n, first_row, band, place, h, s, *refs):
    pieces, middle, outs, rows, back = refs[:n], refs[n], refs[n + 1 : -2], refs[-2], refs[-1]
    j = place[1]
    count = middle.shape[0]
    step = step_of(count)
    unpack_field(place, cuts, count, first_row, band, pieces, rows)

    def body(m, carry):
        state = s[m]
        value = state + 0.5 * step_size * rate(h[m] + rows[pl.ds(m, NB, stride=step), :], state)
        middle[m] = value
        back[pl.ds(m, NB, stride=step), :] = value
        return carry

    lax.fori_loop(0, count, body, 0, unroll=16)
    own = outs[0].shape[1] // LANE
    for k, out in enumerate(outs):
        for a in range(own):
            at = pl.multiple_of(((j ^ k) * own + a) * step, 8)
            out[:, a * LANE : (a + 1) * LANE] = back[pl.ds(at, count), :].astype(bf16)


def second_kernel(ways, spans, start, count, place, h, *refs):
    n = len(spans)
    states, pieces, outs = refs[:n], refs[n : n + ways], refs[n + ways : -2]
    rows, back = refs[-2:]
    j = place[1]
    step = step_of(count)
    unpack_field(place, 1, count, 0, count, pieces, rows)
    for s, (first, low, high) in zip(states, spans):

        def body(m, carry):
            back[pl.ds(m, NB, stride=step), :] = rate(
                h[m] + rows[pl.ds(m, NB, stride=step), :], s[m + (start - first)]
            )
            return carry

        lax.fori_loop(low, high, body, 0, unroll=16)
    own = (outs[0].shape[0] - PACK) // count
    for k, out in enumerate(outs):
        first = (j ^ k) * own
        values = [back[pl.ds(pl.multiple_of((first + a) * step, 8), count), :] for a in range(own)]
        peak = functools.reduce(jnp.maximum, [jnp.abs(v) for v in values])
        codes, power = encode(values, jnp.max(peak, axis=1, keepdims=True))
        for a in range(own):
            out[a * count : (a + 1) * count, :] = codes[a]
        put_power(out, own * count, power)


def last_kernel(chunks, place, *refs):
    states, pieces, (out, done, sems) = refs[: -3 - len(refs[:-3]) * chunks // (1 + chunks)], refs[:-3], refs[-3:]
    ways = len(states)
    pieces = pieces[ways:]
    j = place[1]
    own = states[0].shape[1] // LANE
    count = states[0].shape[0] // chunks
    copies = []
    for c in range(chunks):
        for k in range(ways):
            piece = pieces[c * ways + k]
            here = slice(c * count, (c + 1) * count)
            at = pl.ds(pl.multiple_of(((j ^ k) * chunks + c) * count, count), count)
            spot = (c * ways + k) * count
            scale = get_scale(piece, own * count, count) * step_size

            def block(a):
                code = piece[a * count : (a + 1) * count, :]
                return states[k][here, a * LANE : (a + 1) * LANE] + code.astype(i32).astype(f32) * scale

            for t in range(own // 2):
                real, imag = parts_of(block(2 * t), block(2 * t + 1))
                done[0, spot : spot + count, t * LANE : (t + 1) * LANE] = real
                done[1, spot : spot + count, t * LANE : (t + 1) * LANE] = imag
            copies.append(
                pltpu.make_async_copy(
                    done.at[:, spot : spot + count, :], out.at[:, at, :], sems.at[c * ways + k]
                )
            )
            copies[-1].start()
    for copy in copies:
        copy.wait()


def join_kernel(cuts, *refs):
    pieces, outs = refs[:-cuts], refs[-cuts:]
    count = pieces[0].shape[0]
    at = 0
    for out in outs:
        width = out.shape[1]
        for k, piece in enumerate(pieces):
            out[k * count : (k + 1) * count, :] = piece[:, at : at + width]
        at += width


def tie(values, *others):
    return lax.optimization_barrier((values, others))[0]


def split_rows(own, parts):
    parts = min(parts, own // 2)
    return [2 * ((own // 2 + parts - 1 - n) // parts) for n in range(parts)]


def local(density, h_bands, coupling, donors, counts):
    nka, nb = lax.axis_size("ka"), lax.axis_size("ba")
    i, j = lax.axis_index("ka"), lax.axis_index("ba")
    tiles, mom, pairs = coupling.shape[0], density.shape[1], density.shape[2]
    assert mom == tiles * TILE == REACH * TILE and nka % 2 == 0
    own = pairs // NB
    band = mom // nb
    chunks = 2 if band % 32 == 0 else 1
    count = band // chunks
    sizes1 = [count] * chunks
    place = jnp.stack([i % 2, j, i * tiles]).astype(i32)

    def move(value, target):
        pairs_of = []
        for a in range(nka):
            for b in range(nb):
                ta, tb = target(a, b)
                pairs_of.append((a * nb + b, (ta % nka) * nb + tb))
        return lax.ppermute(value, ("ka", "ba"), pairs_of)

    def in_group(value, k):
        return value if k == 0 else move(value, lambda a, b: (a, b ^ k))

    def across(value):
        return move(value, lambda a, b: (a ^ 1, b))

    def onward(value):
        return move(value, lambda a, b: (a - 2 if a % 2 else a + 2, b))

    def direct(value):
        return move(value, lambda a, b: (a + 1 if a % 2 else a - 1, b))

    shape = jax.ShapeDtypeStruct
    widths = split_rows(own, CUTS)
    cuts = len(widths)
    ecuts = 2 if own % 4 == 0 else 1
    mine = call(round_kernel, [shape((mom, w * LANE), bf16) for w in widths], specs=[VMEM])(density)
    swap = [across(v) for v in mine]
    passed = []
    for q, value in enumerate(swap):
        if q > 0 and q == cuts - 1:
            passed.append(direct(mine[q]))
            continue
        passed.append(onward(value))
    dense = call(
        functools.partial(coupling_kernel, nka * tiles),
        shape((mom, 3 * mom), bf16),
        specs=[SMEM, SMEM, SMEM, VMEM],
    )(place, donors, counts, coupling)
    sent = call(split_kernel, [shape((band, own * LANE), f32)] * nb, n_in=1)(place, density)
    states = [in_group(v, k) for k, v in enumerate(sent)]
    matrices = shape((band, NB, LANE), f32)
    rows = pltpu.VMEM((step_of(band) * NB, LANE), f32)
    hamilton = call(hamilton_kernel, matrices, [rows], specs=[VMEM])(h_bands)
    hamilton, passed[0] = lax.optimization_barrier((hamilton, passed[0]))

    if cuts > 2:
        passed[1] = tie(passed[1], states)
    got, fields = [], []
    for q in range(cuts):
        if q > 1:
            passed[q] = tie(passed[q], got[(q - 2) * nb : (q - 1) * nb])
        fields = call(
            field_one_kernel,
            [shape((widths[q] * band + PACK, LANE), i16)] * nb,
            [pltpu.VMEM((mom, widths[q] * LANE), i16), pltpu.VMEM((mom, LANE), f32)],
            n_in=4,
        )(place, dense, mine[q], swap[q], passed[q])
        got += [in_group(v, k) for k, v in enumerate(fields)]
    state = call(state_kernel, matrices, [rows], n_in=nb)(place, *states)

    chunk_rows = pltpu.VMEM((step_of(count) * NB, LANE), f32)
    chunk_shape = shape((count, NB, LANE), f32)
    middles, parts, spots = [], [], []
    start = 0
    for size in sizes1:
        hc, sc = hamilton[start : start + size], state[start : start + size]
        middle, *outs = call(
            functools.partial(first_kernel, cuts, nb * cuts, start, band),
            [shape((size, NB, LANE), f32)] + [shape((size, own * LANE), bf16)] * nb,
            [pltpu.VMEM((step_of(size) * NB, LANE), f32)] * 2,
            n_in=2 + nb * cuts,
        )(place, hc, sc, *got)
        middles.append((middle, start, size))
        back = [in_group(v, k) for k, v in enumerate(outs)]
        ewidths = [own // 2] * 2 if size > 16 and own % 4 == 0 else [own]
        joined = [shape((nb * size, w * LANE), bf16) for w in ewidths]
        mine = call(functools.partial(join_kernel, len(ewidths)), joined, specs=[VMEM] * nb)(*back)
        for q in range(len(ewidths)):
            swap = across(mine[q])
            last = start + size == band and q == len(ewidths) - 1 and start > 0
            parts += [swap, mine[q], direct(mine[q]) if last else onward(swap)]
            spots += [(b, start, sum(ewidths[:q]) * LANE) for b in range(3)]
        start += size

    pieces = [shape((own * count + PACK, LANE), i16)] * nb
    room = [pltpu.VMEM((nb * count, own * LANE), i16), pltpu.VMEM((nb * count, LANE), f32)]
    *fields, window = call(
        functools.partial(window_field_kernel, spots, 0),
        pieces + [shape((3 * mom, own * LANE), bf16)],
        room,
        n_in=1 + len(parts),
    )(place, dense, *parts)
    for c in range(1, chunks):
        fields += call(functools.partial(field_kernel, c * count), pieces, room, n_in=2)(place, dense, window)
    got = [[in_group(fields[c * nb + k], k) for k in range(nb)] for c in range(chunks)]
    rates = []
    for c in range(chunks):
        start = c * count
        spans = [
            (m, first, max(first, start) - start, min(first + size, start + count) - start)
            for m, first, size in middles
            if first < start + count and first + size > start
        ]
        outs = call(
            functools.partial(second_kernel, nb, [v[1:] for v in spans], start, count),
            pieces,
            [pltpu.VMEM((step_of(count) * NB, LANE), f32)] * 2,
            n_in=1 + len(spans) + nb,
        )(place, hamilton[start : start + count], *[v[0] for v in spans], *got[c])
        rates += [in_group(v, k) for k, v in enumerate(outs)]
    return pl.pallas_call(
        functools.partial(last_kernel, chunks),
        out_shape=shape(density.shape, f32),
        in_specs=[SMEM] + [VMEM] * (nb + nb * chunks),
        out_specs=pl.BlockSpec(memory_space=pl.ANY),
        scratch_shapes=[pltpu.VMEM(density.shape, f32), pltpu.SemaphoreType.DMA((nb * chunks,))],
        compiler_params=pltpu.CompilerParams(vmem_limit_bytes=20 * 2**20),
    )(place, *sent, *rates)


def solution(mesh):
    placed = (
        P(None, "ka", "ba"),
        P(None, ("ka", "ba"), None),
        P("ka", None, None, None),
        P("ka", None),
        P("ka"),
    )
    return jax.shard_map(
        local, mesh=mesh, in_specs=placed, out_specs=P(None, "ka", "ba"), check_vma=False
    )
```

```python
import functools
CUTS = 3

import jax
import jax.numpy as jnp
from jax import lax
from jax.experimental import pallas as pl
from jax.experimental.pallas import tpu as pltpu
from jax.sharding import PartitionSpec as P

NB = 64
TILE = 128
ND = 4
REACH = 2
LANE = 2 * NB
SPAN = (2 * REACH + 1) * TILE
PACK = 16

step_size = 0.25
f32, bf16, i16, i32 = jnp.float32, jnp.bfloat16, jnp.int16, jnp.int32
SMEM = pl.BlockSpec(memory_space=pltpu.SMEM)
VMEM = pl.BlockSpec(memory_space=pltpu.VMEM)


def call(kernel, out, scratch=(), specs=None, n_in=0, work=1.0):
    return pl.pallas_call(
        kernel,
        out_shape=out,
        in_specs=specs if specs is not None else [SMEM] + [VMEM] * n_in,
        scratch_shapes=scratch,
        compiler_params=pltpu.CompilerParams(vmem_limit_bytes=20 * 2**20),
        cost_estimate=pl.CostEstimate(flops=0, bytes_accessed=int(work * 3.6e6), transcendentals=0),
    )


def half_lanes(shape):
    return lax.broadcasted_iota(i32, shape, 1) < NB


def rows_of(real, imag):
    low = half_lanes(real.shape)
    crossed = pltpu.roll(jnp.where(low, imag, real), NB, 1)
    return jnp.where(low, real, crossed), jnp.where(low, crossed, imag)


def parts_of(even, odd):
    low = half_lanes(even.shape)
    crossed = pltpu.roll(jnp.where(low, odd, even), NB, 1)
    return jnp.where(low, even, crossed), jnp.where(low, crossed, odd)


def encode(values, peak):
    power = jnp.ceil(jnp.log2(jnp.maximum(peak, 1e-30)))
    scale = jnp.exp2(15.0 - power)
    codes = [jnp.clip(jnp.round(v * scale), -32767.0, 32767.0).astype(i32).astype(i16) for v in values]
    return codes, power


def own_lane(shape):
    return lax.broadcasted_iota(i32, shape, 0) == lax.broadcasted_iota(i32, shape, 1)


def put_power(out, at, power):
    wide = jnp.where(own_lane((power.shape[0], LANE)), power, 0.0)
    line = jnp.sum(wide, axis=0, keepdims=True)
    out[at : at + PACK, :] = jnp.broadcast_to(line, (PACK, LANE)).astype(i32).astype(i16)


def get_scale(piece, at, count):
    line = piece[at : at + PACK, :].astype(i32).astype(f32)[:1]
    wide = jnp.where(own_lane((count, LANE)), jnp.broadcast_to(line, (count, LANE)), 0.0)
    return jnp.broadcast_to(jnp.exp2(jnp.sum(wide, axis=1, keepdims=True) - 15.0), (count, LANE))


def round_kernel(density, *outs):
    at = 0
    for out in outs:
        for t in range(out.shape[1] // LANE // 2):
            cols = slice(at, at + LANE)
            at += LANE
            even, odd = rows_of(density[0, :, cols], density[1, :, cols])
            out[:, 2 * t * LANE : (2 * t + 1) * LANE] = even.astype(bf16)
            out[:, (2 * t + 1) * LANE : (2 * t + 2) * LANE] = odd.astype(bf16)


def split_kernel(place, density, *outs):
    j = place[1]
    rows = outs[0].shape[0]
    for k, out in enumerate(outs):
        at = pl.ds(pl.multiple_of((j ^ k) * rows, rows), rows)
        for t in range(density.shape[2] // LANE):
            cols = slice(t * LANE, (t + 1) * LANE)
            even, odd = rows_of(density[0, at, cols], density[1, at, cols])
            out[:, 2 * t * LANE : (2 * t + 1) * LANE] = even
            out[:, (2 * t + 1) * LANE : (2 * t + 2) * LANE] = odd


def step_of(count):
    return count + 8


def matrices_from_rows(rows, out):
    count = out.shape[0]

    def body(m, carry):
        out[m] = rows[pl.ds(m, NB, stride=step_of(count)), :]
        return carry

    lax.fori_loop(0, count, body, 0, unroll=8)


def hamilton_kernel(h, out, rows):
    count = out.shape[0]
    for t in range(h.shape[2] // LANE):
        cols = slice(t * LANE, (t + 1) * LANE)
        even, odd = rows_of(h[0, :, cols], h[1, :, cols])
        for a, value in ((2 * t, even), (2 * t + 1, odd)):
            rows[a * step_of(count) : a * step_of(count) + count, :] = value
    matrices_from_rows(rows, out)


def state_kernel(place, *refs):
    pieces, out, rows = refs[:-2], refs[-2], refs[-1]
    j = place[1]
    count = out.shape[0]
    own = pieces[0].shape[1] // LANE
    for k, piece in enumerate(pieces):
        for a in range(own):
            at = pl.multiple_of(((j ^ k) * own + a) * step_of(count), 8)
            rows[pl.ds(at, count), :] = piece[:, a * LANE : (a + 1) * LANE]
    matrices_from_rows(rows, out)


def coupling_kernel(total, place, donors, counts, coupling, out):
    tiles = coupling.shape[0]
    blocks = {}
    for t in range(tiles):
        for o in range(2 * REACH + 1):
            block = jnp.zeros((TILE, TILE), f32)
            for s in range(ND):
                shift = lax.rem(donors[t, s] - (place[2] + t) + REACH + total, total)
                used = jnp.logical_and(shift == o, s < counts[t])
                block = block - coupling[t, s].astype(f32) * jnp.where(used, 1.0, 0.0)
            blocks[t, t + o] = block.astype(bf16)
    empty = jnp.zeros((TILE, TILE), bf16)
    for t in range(tiles):
        for n in range(3 * tiles):
            mirror = (2 - n // tiles) * tiles + n % tiles
            value = jnp.where(place[0] == 1, blocks.get((t, n), empty), blocks.get((t, mirror), empty))
            out[t * TILE : (t + 1) * TILE, n * TILE : (n + 1) * TILE] = value


def field(place, weights, states, codes, powers, outs):
    j = place[1]
    sigma = jnp.dot(weights, states, preferred_element_type=f32)
    (code,), power = encode([sigma], jnp.max(jnp.abs(sigma), axis=1, keepdims=True))
    codes[...] = code
    powers[...] = jnp.broadcast_to(power, powers.shape)
    blocks = codes.shape[1] // LANE
    count = (outs[0].shape[0] - PACK) // blocks
    for k, out in enumerate(outs):
        at = pl.ds(pl.multiple_of((j ^ k) * count, count), count)
        for a in range(blocks):
            out[a * count : (a + 1) * count, :] = codes[at, a * LANE : (a + 1) * LANE]
        put_power(out, blocks * count, powers[at, :1])


def field_one_kernel(place, dense, mine, swap, passed, *refs):
    outs, (codes, powers) = refs[:-2], refs[-2:]
    states = jnp.concatenate([swap[...], mine[...], passed[...]], 0)
    field(place, dense[...], states, codes, powers, outs)


def rows_for(dense, ways, start, count):
    band = dense.shape[0] // ways
    return jnp.concatenate([dense[w * band + start : w * band + start + count, :] for w in range(ways)], 0)


def window_field_kernel(spots, start, place, dense, *refs):
    n = len(spots)
    states, outs, (window, codes, powers) = refs[:n], refs[n:-3], refs[-3:]
    j = place[1]
    ways = len(outs)
    band = window.shape[0] // 3 // ways
    for ref, (b, first, lane) in zip(states, spots):
        count, width = ref.shape[0] // ways, ref.shape[1]
        for k in range(ways):
            at = pl.multiple_of((b * ways + (j ^ k)) * band + first, PACK)
            window[pl.ds(at, count), lane : lane + width] = ref[k * count : (k + 1) * count, :]
    count = codes.shape[0] // ways
    field(place, rows_for(dense, ways, start, count), window[...], codes, powers, outs)


def field_kernel(start, place, dense, window, *refs):
    outs, (codes, powers) = refs[:-2], refs[-2:]
    count = codes.shape[0] // len(outs)
    field(place, rows_for(dense, len(outs), start, count), window[...], codes, powers, outs)


def two_parts(values):
    high = values.astype(bf16)
    return high, (values - high.astype(f32)).astype(bf16)


def turned(rows):
    moved = pltpu.roll(rows, NB, 1)
    return jnp.where(half_lanes(rows.shape), moved, -moved)


def rate(h, s):
    h_high, h_low = two_parts(h)
    s_high, s_low = two_parts(s)
    left = jnp.concatenate(
        [jnp.concatenate([h_high, -s_high], 1), jnp.concatenate([h_low, -s_low], 1)], 0
    )
    right = [
        jnp.concatenate([turned(sp), sp, turned(hp), hp], 0) for sp, hp in ((s_high, h_high), (s_low, h_low))
    ]
    o = jnp.dot(left, jnp.concatenate(right, 1), preferred_element_type=f32)
    return (o[:NB, :LANE] + o[NB:, :LANE]) + (o[:NB, LANE:] + o[NB:, LANE:])


def unpack_field(place, cuts, count, first_row, stride, pieces, rows):
    j = place[1]
    ways = len(pieces) // cuts
    offset = 0
    for q in range(cuts):
        whole = pieces[q * ways].shape[0] - PACK
        own = whole // stride
        for k in range(ways):
            piece = pieces[q * ways + k]
            first = (j ^ k) * (NB // ways) + offset
            scale = get_scale(piece, whole, stride)[first_row : first_row + count]
            for a in range(own):
                at = pl.multiple_of((first + a) * step_of(count), 8)
                code = piece[a * stride + first_row : a * stride + first_row + count, :]
                rows[pl.ds(at, count), :] = code.astype(i32).astype(f32) * scale
        offset += own


def first_kernel(cuts, n, first_row, band, place, h, s, *refs):
    pieces, middle, outs, rows, back = refs[:n], refs[n], refs[n + 1 : -2], refs[-2], refs[-1]
    j = place[1]
    count = middle.shape[0]
    step = step_of(count)
    unpack_field(place, cuts, count, first_row, band, pieces, rows)

    def body(m, carry):
        state = s[m]
        value = state + 0.5 * step_size * rate(h[m] + rows[pl.ds(m, NB, stride=step), :], state)
        middle[m] = value
        back[pl.ds(m, NB, stride=step), :] = value
        return carry

    lax.fori_loop(0, count, body, 0, unroll=True)
    own = outs[0].shape[1] // LANE
    for k, out in enumerate(outs):
        for a in range(own):
            at = pl.multiple_of(((j ^ k) * own + a) * step, 8)
            out[:, a * LANE : (a + 1) * LANE] = back[pl.ds(at, count), :].astype(bf16)


def second_kernel(ways, place, h, s, *refs):
    pieces, outs, rows, back = refs[:ways], refs[ways:-2], refs[-2], refs[-1]
    j = place[1]
    count = h.shape[0]
    step = step_of(count)
    unpack_field(place, 1, count, 0, count, pieces, rows)

    def body(m, carry):
        back[pl.ds(m, NB, stride=step), :] = rate(h[m] + rows[pl.ds(m, NB, stride=step), :], s[m])
        return carry

    lax.fori_loop(0, count, body, 0, unroll=True)
    own = (outs[0].shape[0] - PACK) // count
    for k, out in enumerate(outs):
        first = (j ^ k) * own
        values = [back[pl.ds(pl.multiple_of((first + a) * step, 8), count), :] for a in range(own)]
        peak = functools.reduce(jnp.maximum, [jnp.abs(v) for v in values])
        codes, power = encode(values, jnp.max(peak, axis=1, keepdims=True))
        for a in range(own):
            out[a * count : (a + 1) * count, :] = codes[a]
        put_power(out, own * count, power)


def last_kernel(chunks, place, *refs):
    states, pieces, (out, done, sems) = refs[: -3 - len(refs[:-3]) * chunks // (1 + chunks)], refs[:-3], refs[-3:]
    ways = len(states)
    pieces = pieces[ways:]
    j = place[1]
    own = states[0].shape[1] // LANE
    count = states[0].shape[0] // chunks
    copies = []
    for c in range(chunks):
        for k in range(ways):
            piece = pieces[c * ways + k]
            here = slice(c * count, (c + 1) * count)
            at = pl.ds(pl.multiple_of(((j ^ k) * chunks + c) * count, count), count)
            spot = (c * ways + k) * count
            scale = get_scale(piece, own * count, count) * step_size

            def block(a):
                code = piece[a * count : (a + 1) * count, :]
                return states[k][here, a * LANE : (a + 1) * LANE] + code.astype(i32).astype(f32) * scale

            for t in range(own // 2):
                real, imag = parts_of(block(2 * t), block(2 * t + 1))
                done[0, spot : spot + count, t * LANE : (t + 1) * LANE] = real
                done[1, spot : spot + count, t * LANE : (t + 1) * LANE] = imag
            copies.append(
                pltpu.make_async_copy(
                    done.at[:, spot : spot + count, :], out.at[:, at, :], sems.at[c * ways + k]
                )
            )
            copies[-1].start()
    for copy in copies:
        copy.wait()


def join_kernel(cuts, *refs):
    pieces, outs = refs[:-cuts], refs[-cuts:]
    count = pieces[0].shape[0]
    at = 0
    for out in outs:
        width = out.shape[1]
        for k, piece in enumerate(pieces):
            out[k * count : (k + 1) * count, :] = piece[:, at : at + width]
        at += width


def tie(values, *others):
    return lax.optimization_barrier((values, others))[0]


def split_rows(own, parts):
    parts = min(parts, own // 2)
    return [2 * ((own // 2 + parts - 1 - n) // parts) for n in range(parts)]


def local(density, h_bands, coupling, donors, counts):
    nka, nb = lax.axis_size("ka"), lax.axis_size("ba")
    i, j = lax.axis_index("ka"), lax.axis_index("ba")
    tiles, mom, pairs = coupling.shape[0], density.shape[1], density.shape[2]
    assert mom == tiles * TILE == REACH * TILE and nka % 2 == 0
    own = pairs // NB
    band = mom // nb
    chunks = 2 if band % 32 == 0 else 1
    count = band // chunks
    place = jnp.stack([i % 2, j, i * tiles]).astype(i32)

    def move(value, target):
        pairs_of = []
        for a in range(nka):
            for b in range(nb):
                ta, tb = target(a, b)
                pairs_of.append((a * nb + b, (ta % nka) * nb + tb))
        return lax.ppermute(value, ("ka", "ba"), pairs_of)

    def in_group(value, k):
        return value if k == 0 else move(value, lambda a, b: (a, b ^ k))

    def across(value):
        return move(value, lambda a, b: (a ^ 1, b))

    def onward(value):
        return move(value, lambda a, b: (a - 2 if a % 2 else a + 2, b))

    shape = jax.ShapeDtypeStruct
    widths = split_rows(own, CUTS)
    cuts = len(widths)
    ecuts = 2 if own % 4 == 0 else 1
    mine = call(round_kernel, [shape((mom, w * LANE), bf16) for w in widths], specs=[VMEM])(density)
    swap = [across(v) for v in mine]
    passed = []
    for q, value in enumerate(swap):
        if q > 1:
            value = tie(value, passed[q - 2])
        passed.append(onward(value))
    dense = call(
        functools.partial(coupling_kernel, nka * tiles),
        shape((mom, 3 * mom), bf16),
        specs=[SMEM, SMEM, SMEM, VMEM],
    )(place, donors, counts, coupling)
    sent = call(split_kernel, [shape((band, own * LANE), f32)] * nb, n_in=1)(place, density)
    states = [in_group(v, k) for k, v in enumerate(sent)]
    matrices = shape((band, NB, LANE), f32)
    rows = pltpu.VMEM((step_of(band) * NB, LANE), f32)
    hamilton = call(hamilton_kernel, matrices, [rows], specs=[VMEM])(h_bands)
    hamilton, passed[0] = lax.optimization_barrier((hamilton, passed[0]))

    if cuts > 2:
        passed[1] = tie(passed[1], states)
    got, fields = [], []
    for q in range(cuts):
        if q > 1:
            passed[q] = tie(passed[q], got[(q - 2) * nb : (q - 1) * nb])
        fields = call(
            field_one_kernel,
            [shape((widths[q] * band + PACK, LANE), i16)] * nb,
            [pltpu.VMEM((mom, widths[q] * LANE), i16), pltpu.VMEM((mom, LANE), f32)],
            n_in=4,
        )(place, dense, mine[q], swap[q], passed[q])
        got += [in_group(v, k) for k, v in enumerate(fields)]
    state = call(state_kernel, matrices, [rows], n_in=nb)(place, *states)

    chunk_rows = pltpu.VMEM((step_of(count) * NB, LANE), f32)
    chunk_shape = shape((count, NB, LANE), f32)
    middles, parts, spots = [], [], []
    for c in range(chunks):
        at = slice(c * count, (c + 1) * count)
        hc, sc = hamilton[at], state[at]
        middle, *outs = call(
            functools.partial(first_kernel, cuts, nb * cuts, c * count, band),
            [chunk_shape] + [shape((count, own * LANE), bf16)] * nb,
            [chunk_rows, chunk_rows],
            n_in=2 + nb * cuts,
        )(place, hc, sc, *got)
        middles.append(middle)
        back = [in_group(v, k) for k, v in enumerate(outs)]
        ewidths = [own // ecuts] * ecuts
        joined = [shape((nb * count, w * LANE), bf16) for w in ewidths]
        mine = call(functools.partial(join_kernel, len(ewidths)), joined, specs=[VMEM] * nb)(*back)
        for q in range(len(ewidths)):
            swap = across(mine[q])
            parts += [swap, mine[q], onward(swap)]
            spots += [(b, c * count, sum(ewidths[:q]) * LANE) for b in range(3)]

    pieces = [shape((own * count + PACK, LANE), i16)] * nb
    room = [pltpu.VMEM((nb * count, own * LANE), i16), pltpu.VMEM((nb * count, LANE), f32)]
    *fields, window = call(
        functools.partial(window_field_kernel, spots, 0),
        pieces + [shape((3 * mom, own * LANE), bf16)],
        room,
        n_in=1 + len(parts),
    )(place, dense, *parts)
    for c in range(1, chunks):
        fields += call(functools.partial(field_kernel, c * count), pieces, room, n_in=2)(place, dense, window)
    got = [[in_group(fields[c * nb + k], k) for k in range(nb)] for c in range(chunks)]
    rates = []
    for c in range(chunks):
        hc, sc = hamilton[c * count : (c + 1) * count], middles[c]
        outs = call(
            functools.partial(second_kernel, nb),
            [shape((own * count + PACK, LANE), i16)] * nb,
            [chunk_rows, chunk_rows],
            n_in=2 + nb,
        )(place, hc, sc, *got[c])
        rates += [in_group(v, k) for k, v in enumerate(outs)]
    return pl.pallas_call(
        functools.partial(last_kernel, chunks),
        out_shape=shape(density.shape, f32),
        in_specs=[SMEM] + [VMEM] * (nb + nb * chunks),
        out_specs=pl.BlockSpec(memory_space=pl.ANY),
        scratch_shapes=[pltpu.VMEM(density.shape, f32), pltpu.SemaphoreType.DMA((nb * chunks,))],
        compiler_params=pltpu.CompilerParams(vmem_limit_bytes=20 * 2**20),
    )(place, *sent, *rates)


def solution(mesh):
    placed = (
        P(None, "ka", "ba"),
        P(None, ("ka", "ba"), None),
        P("ka", None, None, None),
        P("ka", None),
        P("ka"),
    )
    return jax.shard_map(
        local, mesh=mesh, in_specs=placed, out_specs=P(None, "ka", "ba"), check_vma=False
    )
```
